32 devices in a mesh: seq: 4 (over y, x), dp: 8 (over z, core).
Axes of the slice: x: 2, y: 2, z: 4, core: 2. Of those that a mesh axis runs over, the one named last changes fastest.
Arguments:
- attn_out: bfloat16 [16384, 3072], P('dp', 'seq'), may hold values from -6 to 6
- cotangent: bfloat16 [16384, 3072], P(('seq', 'dp')), may hold values from -0.09375 to 0.09375
- gate: float32 [8, 3072], P('dp'), may hold values from -4 to 4
- weight: float32 [3072, 3072], P('dp', 'seq'), may hold values from -1.5 to 1.5
- exp_avg: float32 [3072, 3072], P('dp', 'seq'), may hold values from -6 to 6
- exp_avg_sq: float32 [3072, 3072], P('dp', 'seq'), may hold values from 0.25 to 4
- left_stats: float32 [3072, 1536], P('dp', 'seq'), as said below
- right_stats: float32 [6144, 3072], P('dp', 'seq')
- left_basis: float32 [3072, 1536], P('dp', 'seq'), may hold values from -0.3125 to 0.3125
- right_basis: float32 [6144, 3072], P('dp', 'seq'), may hold values from -0.21875 to 0.21875
Outputs:
- update: float32 [3072, 3072], P('dp', 'seq')
- new_weight: float32 [3072, 3072], P('dp', 'seq')
- new_exp_avg: float32 [3072, 3072], P('dp', 'seq')
- new_exp_avg_sq: float32 [3072, 3072], P('dp', 'seq')
- new_left_stats: float32 [3072, 1536], P('dp', 'seq')
- new_right_stats: float32 [6144, 3072], P('dp', 'seq')
The draws below stay inside these ranges and needn't reach their ends.
Inputs may be any that keep to these rules, and one draw needn't show every extreme that they name: Every 384 x 384 block of left_stats and 768 x 768 block of right_stats is symmetric.
All inputs are finite; a program needn't handle non-finite values.
Results may differ from the reference program's by a relative error of at most 0.0003.
Values may be sent and summed in bfloat16 or wider, within the bound.
A program may use at most 128 MiB of HBM per device.

```python
import math
from functools import partial
import jax
import jax.numpy as jnp
from jax import lax

D = 3072
GROUP_TOK = 2048
HD = 3072
TOK_DEV = 512
TOKENS = 16384
LB = 384
HB = 768
N_SEQ = 4
N_DP = 8


def symmetric(key, blocks_down, side, blocks_across):
    drawn = jax.random.normal(key, (blocks_down, side, blocks_across, side), jnp.float32)
    mirrored = 0.5 * (drawn + drawn.transpose(0, 3, 2, 1))
    diagonal = 3.0 * jnp.eye(side, dtype=jnp.float32)[None, :, None, :]
    return (mirrored + diagonal).reshape(blocks_down * side, blocks_across * side)


def draw_left_stats(key, part):
    key = jax.random.fold_in(key, 1)
    return symmetric(key, D // LB, LB, HD // HB)


def draw_right_stats(key, part):
    key = jax.random.fold_in(key, 2)
    return symmetric(key, D // LB, HB, HD // HB)


def with_spikes(values, key, source, target, parts, factor):
    owner, partner = [(jnp.arange(values.shape[position]) // (values.shape[position] // parts)).reshape([-1 if axis == position else 1 for axis in range(values.ndim)]) for position in (source, target)]
    chosen = jax.random.permutation(key, parts)[partner]
    strong = (owner == chosen) | (owner == (partner + parts // 2) % parts)
    return jnp.where(strong, factor * values, values)


def level_of(rng, extent, pieces, smallest, top_value):
    factor_of, own = 1.0, jax.random.fold_in(rng, 6)
    for axis_at, parts in pieces:
        steps = jnp.exp(jax.random.uniform(jax.random.fold_in(own, axis_at), (parts,), jnp.float32, smallest / len(pieces), top_value / len(pieces)))
        factor_of = factor_of * jnp.repeat(steps, extent[axis_at] // parts).reshape([-1 if axis == axis_at else 1 for axis in range(len(extent))])
    return factor_of


def scatter_about(key, extent, scale, bound, cuts=(), kind=jnp.bfloat16):
    values = scale * jax.random.normal(key, extent, jnp.float32)
    if cuts:
        values = values * level_of(key, extent, cuts, -0.22, 0.18)
    return jnp.clip(values, -bound, bound).astype(kind)


def noise_with(own_key, shape, scale, most, split, heavy, held_as=jnp.bfloat16):
    values = scale * jax.random.normal(own_key, shape, jnp.float32)
    if split:
        values = values * level_of(own_key, shape, split, -0.22, 0.18)
    return jnp.clip(with_spikes(values, jax.random.fold_in(own_key, 3), *heavy), -most, most).astype(held_as)


def setup_inputs(seed: int = 0) -> dict:
    arg_keys = jax.random.split(jax.random.key(seed), 11)
    attn_out = scatter_about(arg_keys[0], (TOKENS, HD), 1.0, 6.0, ((0, 8), (1, 4)))
    cotangent = noise_with(arg_keys[1], (TOKENS, D), (1.0 / (GROUP_TOK * N_DP) ** 0.5), 0.09375, ((0, 32),), (0, 1, 32, 2.75))
    gate = scatter_about(arg_keys[2], (N_DP, D), 1.0, 4.0, ((0, 8),), jnp.float32)
    weight = scatter_about(arg_keys[3], (D, HD), 0.25, 1.5, ((0, 8), (1, 4)), jnp.float32)
    exp_avg = scatter_about(arg_keys[4], (D, HD), 1.0, 6.0, ((0, 8), (1, 4)), jnp.float32)
    exp_avg_sq = jnp.clip(jnp.exp(math.log(4.0) - 2.7725887 * jax.random.uniform(arg_keys[5], (D, HD), jnp.float32) ** level_of(arg_keys[5], (D, HD), ((0, 8), (1, 4)), -0.2, 0.2)), 0.25, 4.0)
    left_stats = draw_left_stats(jax.random.fold_in(arg_keys[10], 71), 0)
    right_stats = draw_right_stats(jax.random.fold_in(arg_keys[10], 71), 0)
    left_basis = scatter_about(arg_keys[8], (D, N_SEQ * LB), LB ** -0.5, 0.3125, ((0, 8), (1, 4)), jnp.float32)
    right_basis = scatter_about(arg_keys[9], (N_DP * HB, HD), HB ** -0.5, 0.21875, ((0, 8), (1, 4)), jnp.float32)
    return {"attn_out": attn_out, "cotangent": cotangent, "gate": gate, "weight": weight, "exp_avg": exp_avg, "exp_avg_sq": exp_avg_sq, "left_stats": left_stats, "right_stats": right_stats, "left_basis": left_basis, "right_basis": right_basis}


beta_one = 0.9
beta_two = 0.95
epsilon = 1e-08
learn_rate = 0.02
decay_rate = 0.1

def to_blocks(matrix, height, width):
    return matrix.reshape(N_DP, height, N_SEQ, width).transpose(0, 2, 1, 3)

def from_blocks(blocks_in):
    shaped = blocks_in.transpose(0, 2, 1, 3)
    return shaped.reshape(shaped.shape[0] * shaped.shape[1], shaped.shape[2] * shaped.shape[3])

def reference(attn_out, cotangent, gate, weight, exp_avg, exp_avg_sq, left_stats, right_stats, left_basis, right_basis):
    outs_grouped = attn_out.reshape(N_DP, GROUP_TOK, HD)
    cots_grouped = cotangent.reshape(N_SEQ, N_DP, TOK_DEV, D).transpose(1, 0, 2, 3).reshape(N_DP, GROUP_TOK, D)

    def add_clip(running, inputs):
        clip_out, clip_cot, clip_gate = inputs
        term = lax.dot_general(clip_cot, clip_out, (((0,), (0,)), ((), ())), preferred_element_type=jnp.float32)
        return (running + clip_gate[:, None] * term, None)
    gradient, unused = lax.scan(add_clip, jnp.zeros((D, HD), jnp.float32), (outs_grouped, cots_grouped, gate))
    einsum_hi = partial(jnp.einsum, precision=lax.Precision.HIGHEST)
    grad_b = to_blocks(gradient, LB, HB)
    left_q = to_blocks(left_basis, LB, LB)
    right_q = to_blocks(right_basis, HB, HB)
    left_new = beta_two * to_blocks(left_stats, LB, LB) + (1.0 - beta_two) * einsum_hi('abik,abjk->abij', grad_b, grad_b)
    right_new = beta_two * to_blocks(right_stats, HB, HB) + (1.0 - beta_two) * einsum_hi('abki,abkj->abij', grad_b, grad_b)
    moment = beta_one * to_blocks(exp_avg, LB, HB) + (1.0 - beta_one) * grad_b

    def rotate_in(matrix):
        partial_rot = einsum_hi('abki,abkj->abij', left_q, matrix)
        return einsum_hi('abik,abkj->abij', partial_rot, right_q)
    rotated = rotate_in(grad_b)
    second = beta_two * to_blocks(exp_avg_sq, LB, HB) + (1.0 - beta_two) * rotated * rotated
    direction = rotate_in(moment) / (jnp.sqrt(second) + epsilon)
    partial_back = einsum_hi('abik,abkj->abij', left_q, direction)
    update = einsum_hi('abik,abjk->abij', partial_back, right_q)
    new_weight = to_blocks(weight, LB, HB) * (1.0 - learn_rate * decay_rate) - learn_rate * update
    return (from_blocks(update), from_blocks(new_weight), from_blocks(moment), from_blocks(second), from_blocks(left_new), from_blocks(right_new))
```

```python
import functools

import jax
import jax.numpy as jnp
from jax import lax
from jax.experimental import pallas as pl
from jax.experimental.pallas import tpu as pltpu
from jax.sharding import PartitionSpec as P

beta_one = 0.9
beta_two = 0.95
epsilon = 1e-08
learn_rate = 0.02
decay_rate = 0.1

MESH = pl.DeviceIdType.MESH
BLOCKS = 8
AHEAD = 3


def fine_dot(left_mat, right_mat):
    return jnp.dot(left_mat, right_mat, precision=lax.Precision.HIGH)


def gradient_kernel(
    cot_hbm,
    attn_hbm,
    gate_ref,
    grad_ref,
    gath,
    attn,
    acc,
    pair_out,
    pair_in,
    sums,
    relay_in,
    line_in,
    own_sem,
    attn_sem,
    send_x,
    send_y,
    recv_x,
    recv_y,
    pass_x,
    pass_y,
    diag_x,
    diag_y,
    pair_send,
    pair_recv,
    line_send,
    line_recv,
    relay_recv,
):
    tok = cot_hbm.shape[0]
    half = tok // 2
    rows = grad_ref.shape[0]
    s = lax.axis_index("seq")
    d = lax.axis_index("dp")
    x_peer = s + 1 - 2 * (s % 2)
    y_peer = (s + 2) % 4
    diag = 3 - s
    z, core = d // 2, d % 2
    other = z * 2 + 1 - core
    side = z // 2
    far_end = 3 - 3 * side
    far_mid = 2 - side
    near = side * 4 + 1 - z
    is_end = (z % 3) == 0
    is_mid = (z % 3) != 0

    def block_of(k):
        j, h = k // 2, k % 2
        zj = jnp.where(j == 0, far_end, jnp.where(j == 1, far_mid, jnp.where(j == 2, near, z)))
        cj = jnp.where(h == 0, 1 - core, core)
        return zj * 2 + cj

    def cot_block(k):
        return cot_hbm.at[:, pl.ds(pl.multiple_of(block_of(k) * rows, 128), rows)]

    def part(k, owner, start=0, size=tok):
        return gath.at[k, pl.ds(pl.multiple_of(owner * tok + start, half), size), :]

    def own_copy(k):
        return pltpu.make_async_copy(cot_block(k), part(k, s), own_sem.at[k])

    def remote(src, dst, send, recv, where):
        return pltpu.make_async_remote_copy(
            src_ref=src, dst_ref=dst, send_sem=send, recv_sem=recv, device_id=where, device_id_type=MESH
        )

    def to_x(k):
        return remote(cot_block(k), part(k, s), send_x.at[k], recv_x.at[k], {"seq": x_peer})

    def to_y(k):
        return remote(cot_block(k), part(k, s), send_y.at[k], recv_y.at[k], {"seq": y_peer})

    def relay_y(k):
        piece = part(k, x_peer, 0, half)
        return remote(piece, piece, pass_y.at[k], diag_y.at[k], {"seq": y_peer})

    def relay_x(k):
        piece = part(k, y_peer, half, half)
        return remote(piece, piece, pass_x.at[k], diag_x.at[k], {"seq": x_peer})

    def from_x(k):
        return remote(part(k, x_peer), part(k, x_peer), send_x.at[k], recv_x.at[k], {"seq": x_peer})

    def from_y(k):
        return remote(part(k, y_peer), part(k, y_peer), send_y.at[k], recv_y.at[k], {"seq": y_peer})

    def diag_from_y(k):
        piece = part(k, diag, 0, half)
        return remote(piece, piece, pass_y.at[k], diag_y.at[k], {"seq": y_peer})

    def diag_from_x(k):
        piece = part(k, diag, half, half)
        return remote(piece, piece, pass_x.at[k], diag_x.at[k], {"seq": x_peer})

    def to_other(j):
        return remote(pair_out.at[j], pair_in.at[j], pair_send.at[j], pair_recv.at[j], {"dp": other})

    def line(j, dst, recv, z_to):
        return remote(sums.at[j], dst, line_send.at[j], recv, {"dp": z_to * 2 + core})

    attn_copy = pltpu.make_async_copy(attn_hbm, attn, attn_sem)
    attn_copy.start()

    @pl.loop(0, BLOCKS)
    def _(k):
        own_copy(k).start()

    barrier = pltpu.get_barrier_semaphore()
    for where in (
        {"seq": x_peer},
        {"seq": y_peer},
        {"dp": other},
        {"dp": ((z + 1) % 4) * 2 + core},
        {"dp": ((z + 2) % 4) * 2 + core},
        {"dp": ((z + 3) % 4) * 2 + core},
    ):
        pl.semaphore_signal(barrier, inc=1, device_id=where, device_id_type=MESH)
    pl.semaphore_wait(barrier, 6)

    @pl.loop(0, AHEAD)
    def _(k):
        to_x(k).start()
        to_y(k).start()

    attn_copy.wait()

    def work(k):
        own_copy(k).wait()
        diag_from_y(k).wait_recv()
        diag_from_x(k).wait_recv()
        product = lax.dot_general(
            gath[k], attn[...], (((0,), (0,)), ((), ())), preferred_element_type=jnp.float32
        )
        gate_row = gate_ref[:, pl.ds(pl.multiple_of(block_of(k) * rows, 128), rows)]
        gate_col = jnp.transpose(jnp.broadcast_to(gate_row, (128, rows)))[:, :1]
        acc[...] = product * gate_col
        j, h = k // 2, k % 2

        @pl.when(h == 0)
        def _():
            pair_out[j] = acc[...]
            to_other(j).start()

        @pl.when(h == 1)
        def _():
            to_other(j).wait_recv()

            @pl.when(j < 3)
            def _():
                sums[j] = acc[...] + pair_in[j]

            @pl.when(is_end & (j < 2))
            def _():
                line(j, relay_in.at[j], relay_recv.at[j], near).start()

            @pl.when(j == 2)
            def _():
                line(2, line_in.at[0], line_recv.at[0], near).start()

            @pl.when(is_mid & (j == 1))
            def _():
                line(0, relay_in.at[0], relay_recv.at[0], near).wait_recv()
                sums[0] = sums[0] + relay_in[0]
                line(0, line_in.at[1], line_recv.at[1], far_end).start()

            @pl.when(is_mid & (j == 2))
            def _():
                line(1, relay_in.at[1], relay_recv.at[1], near).wait_recv()
                sums[1] = sums[1] + relay_in[1]
                line(1, line_in.at[1], line_recv.at[1], far_mid).start()

            @pl.when(j == 3)
            def _():
                line(2, line_in.at[0], line_recv.at[0], near).wait_recv()
                line(2, line_in.at[1], line_recv.at[1], near).wait_recv()
                grad_ref[...] = (acc[...] + pair_in[3]) + (line_in[0] + line_in[1])

    @pl.loop(0, BLOCKS + 1)
    def _(k):
        @pl.when(k < BLOCKS)
        def _():
            from_x(k).wait_recv()
            relay_y(k).start()
            from_y(k).wait_recv()
            relay_x(k).start()

        @pl.when(k + AHEAD < BLOCKS)
        def _():
            to_x(k + AHEAD).start()
            to_y(k + AHEAD).start()

        @pl.when(k > 0)
        def _():
            work(k - 1)

    @pl.loop(0, BLOCKS)
    def _(k):
        to_x(k).wait_send()
        to_y(k).wait_send()
        relay_x(k).wait_send()
        relay_y(k).wait_send()

    for j in range(4):
        to_other(j).wait_send()
    for j in range(3):
        line(j, line_in.at[0], line_recv.at[0], near).wait_send()


def fused_gradient(attn_out, cotangent, gate):
    tok, features = cotangent.shape
    all_tok, columns = attn_out.shape
    rows = features // BLOCKS
    dma = pltpu.SemaphoreType.DMA
    block = (rows, columns)
    return pl.pallas_call(
        gradient_kernel,
        out_shape=jax.ShapeDtypeStruct(block, jnp.float32),
        in_specs=[
            pl.BlockSpec(memory_space=pl.ANY),
            pl.BlockSpec(memory_space=pl.ANY),
            pl.BlockSpec(memory_space=pltpu.VMEM),
        ],
        out_specs=pl.BlockSpec(memory_space=pltpu.VMEM),
        scratch_shapes=[
            pltpu.VMEM((BLOCKS, all_tok, rows), jnp.bfloat16),
            pltpu.VMEM((all_tok, columns), jnp.bfloat16),
            pltpu.VMEM(block, jnp.float32),
            pltpu.VMEM((4,) + block, jnp.float32),
            pltpu.VMEM((4,) + block, jnp.float32),
            pltpu.VMEM((3,) + block, jnp.float32),
            pltpu.VMEM((2,) + block, jnp.float32),
            pltpu.VMEM((2,) + block, jnp.float32),
            dma((BLOCKS,)),
            dma,
            dma((BLOCKS,)),
            dma((BLOCKS,)),
            dma((BLOCKS,)),
            dma((BLOCKS,)),
            dma((BLOCKS,)),
            dma((BLOCKS,)),
            dma((BLOCKS,)),
            dma((BLOCKS,)),
            dma((4,)),
            dma((4,)),
            dma((3,)),
            dma((2,)),
            dma((2,)),
        ],
        compiler_params=pltpu.CompilerParams(
            collective_id=0, has_side_effects=True, vmem_limit_bytes=48 * 1024 * 1024
        ),
        cost_estimate=pl.CostEstimate(
            flops=2 * all_tok * features * columns, bytes_accessed=8 * tok * features, transcendentals=0
        ),
    )(cotangent, attn_out, gate)


def plain_gradient(attn_out, cotangent, gate):
    gathered = lax.all_gather(cotangent, "seq", axis=0, tiled=True)
    product = lax.dot_general(
        gathered, attn_out, (((0,), (0,)), ((), ())), preferred_element_type=jnp.float32
    )
    return lax.psum_scatter(gate[0][:, None] * product, "dp", scatter_dimension=0, tiled=True)


def local(
    find_gradient,
    attn_out,
    cotangent,
    gate,
    weight,
    exp_avg,
    exp_avg_sq,
    left_stats,
    right_stats,
    left_basis,
    right_basis,
):
    gradient = find_gradient(attn_out, cotangent, gate)
    left_new = beta_two * left_stats + (1.0 - beta_two) * fine_dot(gradient, gradient.T)
    right_new = beta_two * right_stats + (1.0 - beta_two) * fine_dot(gradient.T, gradient)
    moment = beta_one * exp_avg + (1.0 - beta_one) * gradient

    def rotate_in(matrix):
        return fine_dot(fine_dot(left_basis.T, matrix), right_basis)

    rotated = rotate_in(gradient)
    second = beta_two * exp_avg_sq + (1.0 - beta_two) * rotated * rotated
    direction = rotate_in(moment) / (jnp.sqrt(second) + epsilon)
    update = fine_dot(fine_dot(left_basis, direction), right_basis.T)
    new_weight = weight * (1.0 - learn_rate * decay_rate) - learn_rate * update
    return (update, new_weight, moment, second, left_new, right_new)


def solution(mesh):
    spec = P("dp", "seq")
    in_specs = (spec, P(("seq", "dp"), None), P("dp", None)) + (spec,) * 7
    fits = mesh.shape["seq"] == 4 and mesh.shape["dp"] == BLOCKS
    body = functools.partial(local, fused_gradient if fits else plain_gradient)
    return jax.shard_map(body, mesh=mesh, in_specs=in_specs, out_specs=(spec,) * 6, check_vma=False)
```

```python
import functools

import jax
import jax.numpy as jnp
from jax import lax
from jax.experimental import pallas as pl
from jax.experimental.pallas import tpu as pltpu
from jax.sharding import PartitionSpec as P

beta_one = 0.9
beta_two = 0.95
epsilon = 1e-08
learn_rate = 0.02
decay_rate = 0.1

MESH = pl.DeviceIdType.MESH
BLOCKS = 8
PIECES = 3
AHEAD = 4


def fine_dot(left_mat, right_mat):
    return jnp.dot(left_mat, right_mat, precision=lax.Precision.HIGH)


def halves(value):
    high = value.astype(jnp.bfloat16)
    return high, (value - high.astype(jnp.float32)).astype(jnp.bfloat16)


def three_pass(left, right, dims):
    def one(a, b):
        return lax.dot_general(a, b, (dims, ((), ())), preferred_element_type=jnp.float32)

    return one(left[0], right[0]) + (one(left[0], right[1]) + one(left[1], right[0]))


def gradient_kernel(
    cot_hbm,
    attn_hbm,
    gate_ref,
    mom_hbm,
    left_hbm,
    right_hbm,
    grad_ref,
    turned_ref,
    gath,
    attn,
    acc,
    pair_out,
    pair_in,
    sums,
    relay_in,
    line_in,
    mom,
    left,
    right,
    side_sem,
    own_sem,
    attn_sem,
    send_x,
    send_y,
    recv_x,
    recv_y,
    pass_x,
    pass_y,
    diag_x,
    diag_y,
    pair_send,
    pair_recv,
    line_send,
    line_recv,
    relay_recv,
):
    tok = cot_hbm.shape[0]
    half = tok // 2
    rows = grad_ref.shape[0]
    s = lax.axis_index("seq")
    d = lax.axis_index("dp")
    x_peer = s + 1 - 2 * (s % 2)
    y_peer = (s + 2) % 4
    diag = 3 - s
    z, core = d // 2, d % 2
    other = z * 2 + 1 - core
    side = z // 2
    far_end = 3 - 3 * side
    far_mid = 2 - side
    near = side * 4 + 1 - z
    is_end = (z % 3) == 0
    is_mid = (z % 3) != 0

    def block_of(k):
        j, h = k // 2, k % 2
        zj = jnp.where(j == 0, far_end, jnp.where(j == 1, far_mid, jnp.where(j == 2, near, z)))
        cj = jnp.where(h == 0, 1 - core, core)
        return zj * 2 + cj

    wide = rows // PIECES

    def cot_piece(k):
        start = block_of(k // PIECES) * rows + (k % PIECES) * wide
        return cot_hbm.at[:, pl.ds(pl.multiple_of(start, 128), wide)]

    def part(k, owner, start=0, size=tok):
        return gath.at[
            k // PIECES,
            pl.ds(pl.multiple_of(owner * tok + start, half), size),
            pl.ds(pl.multiple_of((k % PIECES) * wide, 128), wide),
        ]

    def own_copy(k):
        return pltpu.make_async_copy(cot_piece(k), part(k, s), own_sem.at[k])

    def remote(src, dst, send, recv, where):
        return pltpu.make_async_remote_copy(
            src_ref=src, dst_ref=dst, send_sem=send, recv_sem=recv, device_id=where, device_id_type=MESH
        )

    def to_x(k):
        return remote(cot_piece(k), part(k, s), send_x.at[k], recv_x.at[k], {"seq": x_peer})

    def to_y(k):
        return remote(cot_piece(k), part(k, s), send_y.at[k], recv_y.at[k], {"seq": y_peer})

    def relay_y(k):
        piece = part(k, x_peer, 0, half)
        return remote(piece, piece, pass_y.at[k], diag_y.at[k], {"seq": y_peer})

    def relay_x(k):
        piece = part(k, y_peer, half, half)
        return remote(piece, piece, pass_x.at[k], diag_x.at[k], {"seq": x_peer})

    def from_x(k):
        return remote(part(k, x_peer), part(k, x_peer), send_x.at[k], recv_x.at[k], {"seq": x_peer})

    def from_y(k):
        return remote(part(k, y_peer), part(k, y_peer), send_y.at[k], recv_y.at[k], {"seq": y_peer})

    def diag_from_y(k):
        piece = part(k, diag, 0, half)
        return remote(piece, piece, pass_y.at[k], diag_y.at[k], {"seq": y_peer})

    def diag_from_x(k):
        piece = part(k, diag, half, half)
        return remote(piece, piece, pass_x.at[k], diag_x.at[k], {"seq": x_peer})

    def to_other(j):
        return remote(pair_out.at[j], pair_in.at[j], pair_send.at[j], pair_recv.at[j], {"dp": other})

    def line(j, dst, recv, z_to):
        return remote(sums.at[j], dst, line_send.at[j], recv, {"dp": z_to * 2 + core})

    attn_copy = pltpu.make_async_copy(attn_hbm, attn, attn_sem)
    attn_copy.start()
    side_copies = [
        pltpu.make_async_copy(src, dst, side_sem.at[n])
        for n, (src, dst) in enumerate(((mom_hbm, mom), (left_hbm, left), (right_hbm, right)))
    ]
    for copy in side_copies:
        copy.start()
    steps = BLOCKS * PIECES

    @pl.loop(0, steps)
    def _(k):
        own_copy(k).start()

    barrier = pltpu.get_barrier_semaphore()
    for where in (
        {"seq": x_peer},
        {"seq": y_peer},
        {"dp": other},
        {"dp": ((z + 1) % 4) * 2 + core},
        {"dp": ((z + 2) % 4) * 2 + core},
        {"dp": ((z + 3) % 4) * 2 + core},
    ):
        pl.semaphore_signal(barrier, inc=1, device_id=where, device_id_type=MESH)
    pl.semaphore_wait(barrier, 6)

    @pl.loop(0, AHEAD)
    def _(k):
        to_x(k).start()
        to_y(k).start()

    for copy in side_copies:
        copy.wait()
    partial_turn = three_pass(halves(left[...]), halves(mom[...]), ((0,), (0,)))
    turned_ref[...] = three_pass(halves(partial_turn), halves(right[...]), ((1,), (0,)))
    attn_copy.wait()

    def work(k):
        for n in range(PIECES):
            own_copy(k * PIECES + n).wait()
            diag_from_y(k * PIECES + n).wait_recv()
            diag_from_x(k * PIECES + n).wait_recv()
        product = lax.dot_general(
            gath[k], attn[...], (((0,), (0,)), ((), ())), preferred_element_type=jnp.float32
        )
        gate_row = gate_ref[:, pl.ds(pl.multiple_of(block_of(k) * rows, 128), rows)]
        gate_col = jnp.transpose(jnp.broadcast_to(gate_row, (128, rows)))[:, :1]
        acc[...] = product * gate_col
        j, h = k // 2, k % 2

        @pl.when(h == 0)
        def _():
            pair_out[j] = acc[...]
            to_other(j).start()

        @pl.when(h == 1)
        def _():
            to_other(j).wait_recv()

            @pl.when(j < 3)
            def _():
                sums[j] = acc[...] + pair_in[j]

            @pl.when(is_end & (j < 2))
            def _():
                line(j, relay_in.at[j], relay_recv.at[j], near).start()

            @pl.when(j == 2)
            def _():
                line(2, line_in.at[0], line_recv.at[0], near).start()

            @pl.when(is_mid & (j == 1))
            def _():
                line(0, relay_in.at[0], relay_recv.at[0], near).wait_recv()
                sums[0] = sums[0] + relay_in[0]
                line(0, line_in.at[1], line_recv.at[1], far_end).start()

            @pl.when(is_mid & (j == 2))
            def _():
                line(1, relay_in.at[1], relay_recv.at[1], near).wait_recv()
                sums[1] = sums[1] + relay_in[1]
                line(1, line_in.at[1], line_recv.at[1], far_mid).start()

            @pl.when(j == 3)
            def _():
                line(2, line_in.at[0], line_recv.at[0], near).wait_recv()
                line(2, line_in.at[1], line_recv.at[1], near).wait_recv()
                grad_ref[...] = (acc[...] + pair_in[3]) + (line_in[0] + line_in[1])

    @pl.loop(0, steps + 1)
    def _(k):
        @pl.when(k < steps)
        def _():
            from_x(k).wait_recv()
            relay_y(k).start()
            from_y(k).wait_recv()
            relay_x(k).start()

        @pl.when(k + AHEAD < steps)
        def _():
            to_x(k + AHEAD).start()
            to_y(k + AHEAD).start()

        @pl.when((k > 0) & (k % PIECES == 0))
        def _():
            work(k // PIECES - 1)

    @pl.loop(0, steps)
    def _(k):
        to_x(k).wait_send()
        to_y(k).wait_send()
        relay_x(k).wait_send()
        relay_y(k).wait_send()

    for j in range(4):
        to_other(j).wait_send()
    for j in range(3):
        line(j, line_in.at[0], line_recv.at[0], near).wait_send()


def fused_gradient(attn_out, cotangent, gate, exp_avg, left_basis, right_basis):
    tok, features = cotangent.shape
    all_tok, columns = attn_out.shape
    rows = features // BLOCKS
    dma = pltpu.SemaphoreType.DMA
    block = (rows, columns)
    return pl.pallas_call(
        gradient_kernel,
        out_shape=[jax.ShapeDtypeStruct(block, jnp.float32)] * 2,
        in_specs=[
            pl.BlockSpec(memory_space=pl.ANY),
            pl.BlockSpec(memory_space=pl.ANY),
            pl.BlockSpec(memory_space=pltpu.VMEM),
            pl.BlockSpec(memory_space=pl.ANY),
            pl.BlockSpec(memory_space=pl.ANY),
            pl.BlockSpec(memory_space=pl.ANY),
        ],
        out_specs=[pl.BlockSpec(memory_space=pltpu.VMEM)] * 2,
        scratch_shapes=[
            pltpu.VMEM((BLOCKS, all_tok, rows), jnp.bfloat16),
            pltpu.VMEM((all_tok, columns), jnp.bfloat16),
            pltpu.VMEM(block, jnp.float32),
            pltpu.VMEM((4,) + block, jnp.float32),
            pltpu.VMEM((4,) + block, jnp.float32),
            pltpu.VMEM((3,) + block, jnp.float32),
            pltpu.VMEM((2,) + block, jnp.float32),
            pltpu.VMEM((2,) + block, jnp.float32),
            pltpu.VMEM(block, jnp.float32),
            pltpu.VMEM((rows, rows), jnp.float32),
            pltpu.VMEM((columns, columns), jnp.float32),
            dma((3,)),
            dma((BLOCKS * PIECES,)),
            dma,
            dma((BLOCKS * PIECES,)),
            dma((BLOCKS * PIECES,)),
            dma((BLOCKS * PIECES,)),
            dma((BLOCKS * PIECES,)),
            dma((BLOCKS * PIECES,)),
            dma((BLOCKS * PIECES,)),
            dma((BLOCKS * PIECES,)),
            dma((BLOCKS * PIECES,)),
            dma((4,)),
            dma((4,)),
            dma((3,)),
            dma((2,)),
            dma((2,)),
        ],
        compiler_params=pltpu.CompilerParams(
            collective_id=0, has_side_effects=True, vmem_limit_bytes=58 * 1024 * 1024
        ),
        cost_estimate=pl.CostEstimate(
            flops=2 * all_tok * features * columns, bytes_accessed=8 * tok * features, transcendentals=0
        ),
    )(cotangent, attn_out, gate, exp_avg, left_basis, right_basis)


def plain_gradient(attn_out, cotangent, gate, exp_avg, left_basis, right_basis):
    gathered = lax.all_gather(cotangent, "seq", axis=0, tiled=True)
    product = lax.dot_general(
        gathered, attn_out, (((0,), (0,)), ((), ())), preferred_element_type=jnp.float32
    )
    gradient = lax.psum_scatter(gate[0][:, None] * product, "dp", scatter_dimension=0, tiled=True)
    return gradient, fine_dot(fine_dot(left_basis.T, exp_avg), right_basis)


def local(
    find_gradient,
    attn_out,
    cotangent,
    gate,
    weight,
    exp_avg,
    exp_avg_sq,
    left_stats,
    right_stats,
    left_basis,
    right_basis,
):
    gradient, turned = find_gradient(
        attn_out, cotangent, gate, exp_avg, left_basis, right_basis
    )
    left_new = beta_two * left_stats + (1.0 - beta_two) * fine_dot(gradient, gradient.T)
    right_new = beta_two * right_stats + (1.0 - beta_two) * fine_dot(gradient.T, gradient)
    moment = beta_one * exp_avg + (1.0 - beta_one) * gradient
    rotated = fine_dot(fine_dot(left_basis.T, gradient), right_basis)
    second = beta_two * exp_avg_sq + (1.0 - beta_two) * rotated * rotated
    direction = (beta_one * turned + (1.0 - beta_one) * rotated) / (jnp.sqrt(second) + epsilon)
    update = fine_dot(fine_dot(left_basis, direction), right_basis.T)
    new_weight = weight * (1.0 - learn_rate * decay_rate) - learn_rate * update
    return (update, new_weight, moment, second, left_new, right_new)


def solution(mesh):
    spec = P("dp", "seq")
    in_specs = (spec, P(("seq", "dp"), None), P("dp", None)) + (spec,) * 7
    fits = mesh.shape["seq"] == 4 and mesh.shape["dp"] == BLOCKS
    body = functools.partial(local, fused_gradient if fits else plain_gradient)
    return jax.shard_map(body, mesh=mesh, in_specs=in_specs, out_specs=(spec,) * 6, check_vma=False)
```

```python
import functools

import jax
import jax.numpy as jnp
from jax import lax
from jax.experimental import pallas as pl
from jax.experimental.pallas import tpu as pltpu
from jax.sharding import PartitionSpec as P

beta_one = 0.9
beta_two = 0.95
epsilon = 1e-08
learn_rate = 0.02
decay_rate = 0.1

MESH = pl.DeviceIdType.MESH
BLOCKS = 8
PIECES = 3
AHEAD = 4


def fine_dot(left_mat, right_mat):
    return jnp.dot(left_mat, right_mat, precision=lax.Precision.HIGH)


def halves(value):
    high = value.astype(jnp.bfloat16)
    return high, (value - high.astype(jnp.float32)).astype(jnp.bfloat16)


def three_pass(left, right, dims):
    def one(a, b):
        return lax.dot_general(a, b, (dims, ((), ())), preferred_element_type=jnp.float32)

    return one(left[0], right[0]) + (one(left[0], right[1]) + one(left[1], right[0]))


def gradient_kernel(
    cot_hbm,
    attn_hbm,
    gate_ref,
    mom_hbm,
    left_hbm,
    right_hbm,
    grad_ref,
    turned_ref,
    gath,
    attn,
    acc,
    pair_out,
    pair_in,
    sums,
    relay_in,
    line_in,
    mom,
    left,
    right,
    side_sem,
    own_sem,
    attn_sem,
    send_x,
    send_y,
    recv_x,
    recv_y,
    pass_x,
    pass_y,
    diag_x,
    diag_y,
    pair_send,
    pair_recv,
    line_send,
    line_recv,
    relay_recv,
):
    tok = cot_hbm.shape[0]
    half = tok // 2
    rows = grad_ref.shape[0]
    s = lax.axis_index("seq")
    d = lax.axis_index("dp")
    x_peer = s + 1 - 2 * (s % 2)
    y_peer = (s + 2) % 4
    diag = 3 - s
    z, core = d // 2, d % 2
    other = z * 2 + 1 - core
    side = z // 2
    far_end = 3 - 3 * side
    far_mid = 2 - side
    near = side * 4 + 1 - z
    is_end = (z % 3) == 0
    is_mid = (z % 3) != 0

    def block_of(k):
        j, h = k // 2, k % 2
        zj = jnp.where(j == 0, far_end, jnp.where(j == 1, far_mid, jnp.where(j == 2, near, z)))
        cj = jnp.where(h == 0, 1 - core, core)
        return zj * 2 + cj

    wide = rows // PIECES

    def cot_piece(k):
        start = block_of(k // PIECES) * rows + (k % PIECES) * wide
        return cot_hbm.at[:, pl.ds(pl.multiple_of(start, 128), wide)]

    def part(k, owner, start=0, size=tok):
        return gath.at[
            k // PIECES,
            pl.ds(pl.multiple_of(owner * tok + start, half), size),
            pl.ds(pl.multiple_of((k % PIECES) * wide, 128), wide),
        ]

    def own_copy(k):
        return pltpu.make_async_copy(cot_piece(k), part(k, s), own_sem.at[k])

    def remote(src, dst, send, recv, where):
        return pltpu.make_async_remote_copy(
            src_ref=src, dst_ref=dst, send_sem=send, recv_sem=recv, device_id=where, device_id_type=MESH
        )

    def to_x(k):
        return remote(cot_piece(k), part(k, s), send_x.at[k], recv_x.at[k], {"seq": x_peer})

    def to_y(k):
        return remote(cot_piece(k), part(k, s), send_y.at[k], recv_y.at[k], {"seq": y_peer})

    def relay_y(k):
        piece = part(k, x_peer, 0, half)
        return remote(piece, piece, pass_y.at[k], diag_y.at[k], {"seq": y_peer})

    def relay_x(k):
        piece = part(k, y_peer, half, half)
        return remote(piece, piece, pass_x.at[k], diag_x.at[k], {"seq": x_peer})

    def from_x(k):
        return remote(part(k, x_peer), part(k, x_peer), send_x.at[k], recv_x.at[k], {"seq": x_peer})

    def from_y(k):
        return remote(part(k, y_peer), part(k, y_peer), send_y.at[k], recv_y.at[k], {"seq": y_peer})

    def diag_from_y(k):
        piece = part(k, diag, 0, half)
        return remote(piece, piece, pass_y.at[k], diag_y.at[k], {"seq": y_peer})

    def diag_from_x(k):
        piece = part(k, diag, half, half)
        return remote(piece, piece, pass_x.at[k], diag_x.at[k], {"seq": x_peer})

    def to_other(j):
        return remote(pair_out.at[j], pair_in.at[j], pair_send.at[j], pair_recv.at[j], {"dp": other})

    def line(j, dst, recv, z_to):
        return remote(sums.at[j], dst, line_send.at[j], recv, {"dp": z_to * 2 + core})

    attn_copy = pltpu.make_async_copy(attn_hbm, attn, attn_sem)
    attn_copy.start()
    side_copies = [
        pltpu.make_async_copy(src, dst, side_sem.at[n])
        for n, (src, dst) in enumerate(((mom_hbm, mom), (left_hbm, left), (right_hbm, right)))
    ]
    for copy in side_copies:
        copy.start()
    steps = BLOCKS * PIECES

    @pl.loop(0, steps)
    def _(k):
        own_copy(k).start()

    barrier = pltpu.get_barrier_semaphore()
    for where in (
        {"seq": x_peer},
        {"seq": y_peer},
        {"dp": other},
        {"dp": ((z + 1) % 4) * 2 + core},
        {"dp": ((z + 2) % 4) * 2 + core},
        {"dp": ((z + 3) % 4) * 2 + core},
    ):
        pl.semaphore_signal(barrier, inc=1, device_id=where, device_id_type=MESH)
    pl.semaphore_wait(barrier, 6)

    @pl.loop(0, AHEAD)
    def _(k):
        to_x(k).start()
        to_y(k).start()

    for copy in side_copies:
        copy.wait()
    partial_turn = three_pass(halves(left[...]), halves(mom[...]), ((0,), (0,)))
    turned_ref[...] = three_pass(halves(partial_turn), halves(right[...]), ((1,), (0,)))
    attn_copy.wait()

    def work(k):
        for n in range(PIECES):
            own_copy(k * PIECES + n).wait()
            diag_from_y(k * PIECES + n).wait_recv()
            diag_from_x(k * PIECES + n).wait_recv()
        product = lax.dot_general(
            gath[k], attn[...], (((0,), (0,)), ((), ())), preferred_element_type=jnp.float32
        )
        gate_row = gate_ref[:, pl.ds(pl.multiple_of(block_of(k) * rows, 128), rows)]
        gate_col = jnp.transpose(jnp.broadcast_to(gate_row, (128, rows)))[:, :1]
        acc[...] = product * gate_col
        j, h = k // 2, k % 2

        @pl.when(h == 0)
        def _():
            pair_out[j] = acc[...]
            to_other(j).start()

        @pl.when(h == 1)
        def _():
            to_other(j).wait_recv()

            @pl.when(j < 3)
            def _():
                sums[j] = acc[...] + pair_in[j]

            @pl.when(is_end & (j < 2))
            def _():
                line(j, relay_in.at[j], relay_recv.at[j], near).start()

            @pl.when(j == 2)
            def _():
                line(2, line_in.at[0], line_recv.at[0], near).start()

            @pl.when(is_mid & (j == 1))
            def _():
                line(0, relay_in.at[0], relay_recv.at[0], near).wait_recv()
                sums[0] = sums[0] + relay_in[0]
                line(0, line_in.at[1], line_recv.at[1], far_end).start()

            @pl.when(is_mid & (j == 2))
            def _():
                line(1, relay_in.at[1], relay_recv.at[1], near).wait_recv()
                sums[1] = sums[1] + relay_in[1]
                line(1, line_in.at[1], line_recv.at[1], far_mid).start()

            @pl.when(j == 3)
            def _():
                line(2, line_in.at[0], line_recv.at[0], near).wait_recv()
                line(2, line_in.at[1], line_recv.at[1], near).wait_recv()
                grad_ref[...] = (acc[...] + pair_in[3]) + (line_in[0] + line_in[1])

    @pl.loop(0, steps + 1)
    def _(k):
        @pl.when(k < steps)
        def _():
            from_x(k).wait_recv()
            relay_y(k).start()
            from_y(k).wait_recv()
            relay_x(k).start()

        @pl.when(k + AHEAD < steps)
        def _():
            to_x(k + AHEAD).start()
            to_y(k + AHEAD).start()

        @pl.when((k > 0) & (k % PIECES == 0))
        def _():
            work(k // PIECES - 1)

    @pl.loop(0, steps)
    def _(k):
        to_x(k).wait_send()
        to_y(k).wait_send()
        relay_x(k).wait_send()
        relay_y(k).wait_send()

    for j in range(4):
        to_other(j).wait_send()
    for j in range(3):
        line(j, line_in.at[0], line_recv.at[0], near).wait_send()


def fused_gradient(attn_out, cotangent, gate, exp_avg, left_basis, right_basis):
    tok, features = cotangent.shape
    all_tok, columns = attn_out.shape
    rows = features // BLOCKS
    dma = pltpu.SemaphoreType.DMA
    block = (rows, columns)
    return pl.pallas_call(
        gradient_kernel,
        out_shape=[jax.ShapeDtypeStruct(block, jnp.float32)] * 2,
        in_specs=[
            pl.BlockSpec(memory_space=pl.ANY),
            pl.BlockSpec(memory_space=pl.ANY),
            pl.BlockSpec(memory_space=pltpu.VMEM),
            pl.BlockSpec(memory_space=pl.ANY),
            pl.BlockSpec(memory_space=pl.ANY),
            pl.BlockSpec(memory_space=pl.ANY),
        ],
        out_specs=[pl.BlockSpec(memory_space=pltpu.VMEM)] * 2,
        scratch_shapes=[
            pltpu.VMEM((BLOCKS, all_tok, rows), jnp.bfloat16),
            pltpu.VMEM((all_tok, columns), jnp.bfloat16),
            pltpu.VMEM(block, jnp.float32),
            pltpu.VMEM((4,) + block, jnp.float32),
            pltpu.VMEM((4,) + block, jnp.float32),
            pltpu.VMEM((3,) + block, jnp.float32),
            pltpu.VMEM((2,) + block, jnp.float32),
            pltpu.VMEM((2,) + block, jnp.float32),
            pltpu.VMEM(block, jnp.float32),
            pltpu.VMEM((rows, rows), jnp.float32),
            pltpu.VMEM((columns, columns), jnp.float32),
            dma((3,)),
            dma((BLOCKS * PIECES,)),
            dma,
            dma((BLOCKS * PIECES,)),
            dma((BLOCKS * PIECES,)),
            dma((BLOCKS * PIECES,)),
            dma((BLOCKS * PIECES,)),
            dma((BLOCKS * PIECES,)),
            dma((BLOCKS * PIECES,)),
            dma((BLOCKS * PIECES,)),
            dma((BLOCKS * PIECES,)),
            dma((4,)),
            dma((4,)),
            dma((3,)),
            dma((2,)),
            dma((2,)),
        ],
        compiler_params=pltpu.CompilerParams(
            collective_id=0, has_side_effects=True, vmem_limit_bytes=58 * 1024 * 1024
        ),
        cost_estimate=pl.CostEstimate(
            flops=2 * all_tok * features * columns, bytes_accessed=8 * tok * features, transcendentals=0
        ),
    )(cotangent, attn_out, gate, exp_avg, left_basis, right_basis)


def finish_kernel(grad_ref, turned_ref, *refs):
    sources, targets = refs[:7], refs[7:13]
    weight, exp_avg, exp_sq, left_old, right_old, left, right = held = refs[13:20]
    update, weight_new, moment, second, left_new, right_new = made = refs[20:26]
    in_sem, out_sem = refs[26:]
    arrive = [pltpu.make_async_copy(sources[n], held[n], in_sem.at[n]) for n in range(7)]
    leave = [pltpu.make_async_copy(made[n], targets[n], out_sem.at[n]) for n in range(6)]
    for n in (4, 3, 5, 6, 1, 2, 0):
        arrive[n].start()
    grad = grad_ref[...]
    grad_h = halves(grad)
    right_gram = three_pass(grad_h, grad_h, ((0,), (0,)))
    arrive[4].wait()
    right_new[...] = beta_two * right_old[...] + (1.0 - beta_two) * right_gram
    leave[5].start()
    left_gram = three_pass(grad_h, grad_h, ((1,), (1,)))
    arrive[3].wait()
    left_new[...] = beta_two * left_old[...] + (1.0 - beta_two) * left_gram
    leave[4].start()
    arrive[1].wait()
    moment[...] = beta_one * exp_avg[...] + (1.0 - beta_one) * grad
    leave[2].start()
    arrive[5].wait()
    left_h = halves(left[...])
    partial_in = three_pass(left_h, grad_h, ((0,), (0,)))
    arrive[6].wait()
    right_h = halves(right[...])
    rotated = three_pass(halves(partial_in), right_h, ((1,), (0,)))
    arrive[2].wait()
    second[...] = beta_two * exp_sq[...] + (1.0 - beta_two) * rotated * rotated
    leave[3].start()
    turned = beta_one * turned_ref[...] + (1.0 - beta_one) * rotated
    direction = turned / (jnp.sqrt(second[...]) + epsilon)
    partial_back = three_pass(left_h, halves(direction), ((1,), (0,)))
    update[...] = three_pass(halves(partial_back), right_h, ((1,), (1,)))
    leave[0].start()
    arrive[0].wait()
    weight_new[...] = weight[...] * (1.0 - learn_rate * decay_rate) - learn_rate * update[...]
    leave[1].start()
    for copy in leave:
        copy.wait()


def fused_finish(gradient, turned, *arrays):
    weight, left_stats, right_stats = arrays[0], arrays[3], arrays[4]
    shapes = [weight.shape] * 4 + [left_stats.shape, right_stats.shape]
    spaces = [pltpu.VMEM(array.shape, jnp.float32) for array in arrays]
    spaces += [pltpu.VMEM(shape, jnp.float32) for shape in shapes]
    return pl.pallas_call(
        finish_kernel,
        out_shape=[jax.ShapeDtypeStruct(shape, jnp.float32) for shape in shapes],
        in_specs=[pl.BlockSpec(memory_space=pltpu.VMEM)] * 2 + [pl.BlockSpec(memory_space=pl.ANY)] * 7,
        out_specs=[pl.BlockSpec(memory_space=pl.ANY)] * 6,
        scratch_shapes=spaces + [pltpu.SemaphoreType.DMA((7,)), pltpu.SemaphoreType.DMA((6,))],
        compiler_params=pltpu.CompilerParams(vmem_limit_bytes=52 * 1024 * 1024),
    )(gradient, turned, *arrays)


def plain_gradient(attn_out, cotangent, gate, exp_avg, left_basis, right_basis):
    gathered = lax.all_gather(cotangent, "seq", axis=0, tiled=True)
    product = lax.dot_general(
        gathered, attn_out, (((0,), (0,)), ((), ())), preferred_element_type=jnp.float32
    )
    gradient = lax.psum_scatter(gate[0][:, None] * product, "dp", scatter_dimension=0, tiled=True)
    return gradient, fine_dot(fine_dot(left_basis.T, exp_avg), right_basis)


def plain_finish(
    gradient,
    turned,
    weight,
    exp_avg,
    exp_avg_sq,
    left_stats,
    right_stats,
    left_basis,
    right_basis,
):
    left_new = beta_two * left_stats + (1.0 - beta_two) * fine_dot(gradient, gradient.T)
    right_new = beta_two * right_stats + (1.0 - beta_two) * fine_dot(gradient.T, gradient)
    moment = beta_one * exp_avg + (1.0 - beta_one) * gradient
    rotated = fine_dot(fine_dot(left_basis.T, gradient), right_basis)
    second = beta_two * exp_avg_sq + (1.0 - beta_two) * rotated * rotated
    direction = (beta_one * turned + (1.0 - beta_one) * rotated) / (jnp.sqrt(second) + epsilon)
    update = fine_dot(fine_dot(left_basis, direction), right_basis.T)
    new_weight = weight * (1.0 - learn_rate * decay_rate) - learn_rate * update
    return (update, new_weight, moment, second, left_new, right_new)


def local(fits, attn_out, cotangent, gate, *arrays):
    exp_avg, left_basis, right_basis = arrays[1], arrays[5], arrays[6]
    find = fused_gradient if fits else plain_gradient
    gradient, turned = find(attn_out, cotangent, gate, exp_avg, left_basis, right_basis)
    finish = fused_finish if fits else plain_finish
    return tuple(finish(gradient, turned, *arrays))


def solution(mesh):
    spec = P("dp", "seq")
    in_specs = (spec, P(("seq", "dp"), None), P("dp", None)) + (spec,) * 7
    fits = mesh.shape["seq"] == 4 and mesh.shape["dp"] == BLOCKS
    body = functools.partial(local, fits)
    return jax.shard_map(body, mesh=mesh, in_specs=in_specs, out_specs=(spec,) * 6, check_vma=False)
```

```python
import functools

import jax
import jax.numpy as jnp
from jax import lax
from jax.experimental import pallas as pl
from jax.experimental.pallas import tpu as pltpu
from jax.sharding import PartitionSpec as P

beta_one = 0.9
beta_two = 0.95
epsilon = 1e-08
learn_rate = 0.02
decay_rate = 0.1

MESH = pl.DeviceIdType.MESH
BLOCKS = 8
PIECES = 3
AHEAD = 7


def fine_dot(left_mat, right_mat):
    return jnp.dot(left_mat, right_mat, precision=lax.Precision.HIGH)


def halves(value):
    high = value.astype(jnp.bfloat16)
    return high, (value - high.astype(jnp.float32)).astype(jnp.bfloat16)


def three_pass(left, right, dims):
    def one(a, b):
        return lax.dot_general(a, b, (dims, ((), ())), preferred_element_type=jnp.float32)

    return one(left[0], right[0]) + (one(left[0], right[1]) + one(left[1], right[0]))


def gradient_kernel(
    cot_hbm,
    attn_hbm,
    gate_ref,
    mom_hbm,
    left_hbm,
    right_hbm,
    grad_ref,
    turned_ref,
    gath,
    attn,
    acc,
    pair_out,
    pair_in,
    sums,
    relay_in,
    line_in,
    mom,
    left,
    right,
    side_sem,
    own_sem,
    attn_sem,
    send_x,
    send_y,
    recv_x,
    recv_y,
    pass_x,
    pass_y,
    diag_x,
    diag_y,
    pair_send,
    pair_recv,
    line_send,
    line_recv,
    relay_recv,
):
    tok = cot_hbm.shape[0]
    half = tok // 2
    rows = grad_ref.shape[0]
    s = lax.axis_index("seq")
    d = lax.axis_index("dp")
    x_peer = s + 1 - 2 * (s % 2)
    y_peer = (s + 2) % 4
    diag = 3 - s
    z, core = d // 2, d % 2
    other = z * 2 + 1 - core
    side = z // 2
    far_end = 3 - 3 * side
    far_mid = 2 - side
    near = side * 4 + 1 - z
    is_end = (z % 3) == 0
    is_mid = (z % 3) != 0

    def block_of(k):
        j, h = k // 2, k % 2
        zj = jnp.where(j == 0, far_end, jnp.where(j == 1, far_mid, jnp.where(j == 2, near, z)))
        cj = jnp.where(h == 0, 1 - core, core)
        return zj * 2 + cj

    wide = rows // PIECES

    def cot_piece(k):
        start = block_of(k // PIECES) * rows + (k % PIECES) * wide
        return cot_hbm.at[:, pl.ds(pl.multiple_of(start, 128), wide)]

    def part(k, owner, start=0, size=tok):
        return gath.at[
            k // PIECES,
            pl.ds(pl.multiple_of(owner * tok + start, half), size),
            pl.ds(pl.multiple_of((k % PIECES) * wide, 128), wide),
        ]

    def own_copy(k):
        return pltpu.make_async_copy(cot_piece(k), part(k, s), own_sem.at[k])

    def remote(src, dst, send, recv, where):
        return pltpu.make_async_remote_copy(
            src_ref=src, dst_ref=dst, send_sem=send, recv_sem=recv, device_id=where, device_id_type=MESH
        )

    def to_x(k):
        return remote(cot_piece(k), part(k, s), send_x.at[k], recv_x.at[k], {"seq": x_peer})

    def to_y(k):
        return remote(cot_piece(k), part(k, s), send_y.at[k], recv_y.at[k], {"seq": y_peer})

    def relay_y(k):
        piece = part(k, x_peer, 0, half)
        return remote(piece, piece, pass_y.at[k], diag_y.at[k], {"seq": y_peer})

    def relay_x(k):
        piece = part(k, y_peer, half, half)
        return remote(piece, piece, pass_x.at[k], diag_x.at[k], {"seq": x_peer})

    def from_x(k):
        return remote(part(k, x_peer), part(k, x_peer), send_x.at[k], recv_x.at[k], {"seq": x_peer})

    def from_y(k):
        return remote(part(k, y_peer), part(k, y_peer), send_y.at[k], recv_y.at[k], {"seq": y_peer})

    def diag_from_y(k):
        piece = part(k, diag, 0, half)
        return remote(piece, piece, pass_y.at[k], diag_y.at[k], {"seq": y_peer})

    def diag_from_x(k):
        piece = part(k, diag, half, half)
        return remote(piece, piece, pass_x.at[k], diag_x.at[k], {"seq": x_peer})

    def to_other(j):
        return remote(pair_out.at[j], pair_in.at[j], pair_send.at[j], pair_recv.at[j], {"dp": other})

    def line(j, dst, recv, z_to):
        return remote(sums.at[j], dst, line_send.at[j], recv, {"dp": z_to * 2 + core})

    attn_copy = pltpu.make_async_copy(attn_hbm, attn, attn_sem)
    attn_copy.start()
    side_copies = [
        pltpu.make_async_copy(src, dst, side_sem.at[n])
        for n, (src, dst) in enumerate(((mom_hbm, mom), (left_hbm, left), (right_hbm, right)))
    ]
    for copy in side_copies:
        copy.start()
    steps = BLOCKS * PIECES

    @pl.loop(0, steps)
    def _(k):
        own_copy(k).start()

    barrier = pltpu.get_barrier_semaphore()
    for where in (
        {"seq": x_peer},
        {"seq": y_peer},
        {"dp": other},
        {"dp": ((z + 1) % 4) * 2 + core},
        {"dp": ((z + 2) % 4) * 2 + core},
        {"dp": ((z + 3) % 4) * 2 + core},
    ):
        pl.semaphore_signal(barrier, inc=1, device_id=where, device_id_type=MESH)
    pl.semaphore_wait(barrier, 6)

    @pl.loop(0, AHEAD)
    def _(k):
        to_x(k).start()
        to_y(k).start()

    for copy in side_copies:
        copy.wait()
    partial_turn = three_pass(halves(left[...]), halves(mom[...]), ((0,), (0,)))
    turned_ref[...] = three_pass(halves(partial_turn), halves(right[...]), ((1,), (0,)))
    attn_copy.wait()

    def work(k):
        for n in range(PIECES):
            own_copy(k * PIECES + n).wait()
            diag_from_y(k * PIECES + n).wait_recv()
            diag_from_x(k * PIECES + n).wait_recv()
        product = lax.dot_general(
            gath[k], attn[...], (((0,), (0,)), ((), ())), preferred_element_type=jnp.float32
        )
        gate_row = gate_ref[:, pl.ds(pl.multiple_of(block_of(k) * rows, 128), rows)]
        gate_col = jnp.transpose(jnp.broadcast_to(gate_row, (128, rows)))[:, :1]
        acc[...] = product * gate_col
        j, h = k // 2, k % 2

        @pl.when(h == 0)
        def _():
            pair_out[j] = acc[...]
            to_other(j).start()

        @pl.when(h == 1)
        def _():
            to_other(j).wait_recv()

            @pl.when(j < 3)
            def _():
                sums[j] = acc[...] + pair_in[j]

            @pl.when(is_end & (j < 2))
            def _():
                line(j, relay_in.at[j], relay_recv.at[j], near).start()

            @pl.when(j == 2)
            def _():
                line(2, line_in.at[0], line_recv.at[0], near).start()

            @pl.when(is_mid & (j == 1))
            def _():
                line(0, relay_in.at[0], relay_recv.at[0], near).wait_recv()
                sums[0] = sums[0] + relay_in[0]
                line(0, line_in.at[1], line_recv.at[1], far_end).start()

            @pl.when(is_mid & (j == 2))
            def _():
                line(1, relay_in.at[1], relay_recv.at[1], near).wait_recv()
                sums[1] = sums[1] + relay_in[1]
                line(1, line_in.at[1], line_recv.at[1], far_mid).start()

            @pl.when(j == 3)
            def _():
                line(2, line_in.at[0], line_recv.at[0], near).wait_recv()
                line(2, line_in.at[1], line_recv.at[1], near).wait_recv()
                grad_ref[...] = (acc[...] + pair_in[3]) + (line_in[0] + line_in[1])

    @pl.loop(0, steps + 1)
    def _(k):
        @pl.when(k < steps)
        def _():
            from_x(k).wait_recv()
            relay_y(k).start()
            from_y(k).wait_recv()
            relay_x(k).start()

        @pl.when(k + AHEAD < steps)
        def _():
            to_x(k + AHEAD).start()
            to_y(k + AHEAD).start()

        @pl.when((k > 0) & (k % PIECES == 0))
        def _():
            work(k // PIECES - 1)

    @pl.loop(0, steps)
    def _(k):
        to_x(k).wait_send()
        to_y(k).wait_send()
        relay_x(k).wait_send()
        relay_y(k).wait_send()

    for j in range(4):
        to_other(j).wait_send()
    for j in range(3):
        line(j, line_in.at[0], line_recv.at[0], near).wait_send()


def fused_gradient(attn_out, cotangent, gate, exp_avg, left_basis, right_basis):
    tok, features = cotangent.shape
    all_tok, columns = attn_out.shape
    rows = features // BLOCKS
    dma = pltpu.SemaphoreType.DMA
    block = (rows, columns)
    return pl.pallas_call(
        gradient_kernel,
        out_shape=[jax.ShapeDtypeStruct(block, jnp.float32)] * 2,
        in_specs=[
            pl.BlockSpec(memory_space=pl.ANY),
            pl.BlockSpec(memory_space=pl.ANY),
            pl.BlockSpec(memory_space=pltpu.VMEM),
            pl.BlockSpec(memory_space=pl.ANY),
            pl.BlockSpec(memory_space=pl.ANY),
            pl.BlockSpec(memory_space=pl.ANY),
        ],
        out_specs=[pl.BlockSpec(memory_space=pltpu.VMEM)] * 2,
        scratch_shapes=[
            pltpu.VMEM((BLOCKS, all_tok, rows), jnp.bfloat16),
            pltpu.VMEM((all_tok, columns), jnp.bfloat16),
            pltpu.VMEM(block, jnp.float32),
            pltpu.VMEM((4,) + block, jnp.float32),
            pltpu.VMEM((4,) + block, jnp.float32),
            pltpu.VMEM((3,) + block, jnp.float32),
            pltpu.VMEM((2,) + block, jnp.float32),
            pltpu.VMEM((2,) + block, jnp.float32),
            pltpu.VMEM(block, jnp.float32),
            pltpu.VMEM((rows, rows), jnp.float32),
            pltpu.VMEM((columns, columns), jnp.float32),
            dma((3,)),
            dma((BLOCKS * PIECES,)),
            dma,
            dma((BLOCKS * PIECES,)),
            dma((BLOCKS * PIECES,)),
            dma((BLOCKS * PIECES,)),
            dma((BLOCKS * PIECES,)),
            dma((BLOCKS * PIECES,)),
            dma((BLOCKS * PIECES,)),
            dma((BLOCKS * PIECES,)),
            dma((BLOCKS * PIECES,)),
            dma((4,)),
            dma((4,)),
            dma((3,)),
            dma((2,)),
            dma((2,)),
        ],
        compiler_params=pltpu.CompilerParams(
            collective_id=0, has_side_effects=True, vmem_limit_bytes=58 * 1024 * 1024
        ),
        cost_estimate=pl.CostEstimate(
            flops=2 * all_tok * features * columns, bytes_accessed=8 * tok * features, transcendentals=0
        ),
    )(cotangent, attn_out, gate, exp_avg, left_basis, right_basis)


def finish_kernel(grad_ref, turned_ref, *refs):
    sources, targets = refs[:7], refs[7:13]
    weight, exp_avg, exp_sq, left_old, right_old, left, right = held = refs[13:20]
    update, weight_new, moment, second, left_new, right_new = made = refs[20:26]
    in_sem, out_sem = refs[26:]
    arrive = [pltpu.make_async_copy(sources[n], held[n], in_sem.at[n]) for n in range(7)]
    leave = [pltpu.make_async_copy(made[n], targets[n], out_sem.at[n]) for n in range(6)]
    for n in (4, 3, 5, 6, 1, 2, 0):
        arrive[n].start()
    grad = grad_ref[...]
    grad_h = halves(grad)
    right_gram = three_pass(grad_h, grad_h, ((0,), (0,)))
    arrive[4].wait()
    right_new[...] = beta_two * right_old[...] + (1.0 - beta_two) * right_gram
    leave[5].start()
    left_gram = three_pass(grad_h, grad_h, ((1,), (1,)))
    arrive[3].wait()
    left_new[...] = beta_two * left_old[...] + (1.0 - beta_two) * left_gram
    leave[4].start()
    arrive[1].wait()
    moment[...] = beta_one * exp_avg[...] + (1.0 - beta_one) * grad
    leave[2].start()
    arrive[5].wait()
    left_h = halves(left[...])
    partial_in = three_pass(left_h, grad_h, ((0,), (0,)))
    arrive[6].wait()
    right_h = halves(right[...])
    rotated = three_pass(halves(partial_in), right_h, ((1,), (0,)))
    arrive[2].wait()
    second[...] = beta_two * exp_sq[...] + (1.0 - beta_two) * rotated * rotated
    leave[3].start()
    turned = beta_one * turned_ref[...] + (1.0 - beta_one) * rotated
    direction = turned / (jnp.sqrt(second[...]) + epsilon)
    partial_back = three_pass(left_h, halves(direction), ((1,), (0,)))
    update[...] = three_pass(halves(partial_back), right_h, ((1,), (1,)))
    leave[0].start()
    arrive[0].wait()
    weight_new[...] = weight[...] * (1.0 - learn_rate * decay_rate) - learn_rate * update[...]
    leave[1].start()
    for copy in leave:
        copy.wait()


def fused_finish(gradient, turned, *arrays):
    weight, left_stats, right_stats = arrays[0], arrays[3], arrays[4]
    shapes = [weight.shape] * 4 + [left_stats.shape, right_stats.shape]
    spaces = [pltpu.VMEM(array.shape, jnp.float32) for array in arrays]
    spaces += [pltpu.VMEM(shape, jnp.float32) for shape in shapes]
    return pl.pallas_call(
        finish_kernel,
        out_shape=[jax.ShapeDtypeStruct(shape, jnp.float32) for shape in shapes],
        in_specs=[pl.BlockSpec(memory_space=pltpu.VMEM)] * 2 + [pl.BlockSpec(memory_space=pl.ANY)] * 7,
        out_specs=[pl.BlockSpec(memory_space=pl.ANY)] * 6,
        scratch_shapes=spaces + [pltpu.SemaphoreType.DMA((7,)), pltpu.SemaphoreType.DMA((6,))],
        compiler_params=pltpu.CompilerParams(vmem_limit_bytes=52 * 1024 * 1024),
    )(gradient, turned, *arrays)


def plain_gradient(attn_out, cotangent, gate, exp_avg, left_basis, right_basis):
    gathered = lax.all_gather(cotangent, "seq", axis=0, tiled=True)
    product = lax.dot_general(
        gathered, attn_out, (((0,), (0,)), ((), ())), preferred_element_type=jnp.float32
    )
    gradient = lax.psum_scatter(gate[0][:, None] * product, "dp", scatter_dimension=0, tiled=True)
    return gradient, fine_dot(fine_dot(left_basis.T, exp_avg), right_basis)


def plain_finish(
    gradient,
    turned,
    weight,
    exp_avg,
    exp_avg_sq,
    left_stats,
    right_stats,
    left_basis,
    right_basis,
):
    left_new = beta_two * left_stats + (1.0 - beta_two) * fine_dot(gradient, gradient.T)
    right_new = beta_two * right_stats + (1.0 - beta_two) * fine_dot(gradient.T, gradient)
    moment = beta_one * exp_avg + (1.0 - beta_one) * gradient
    rotated = fine_dot(fine_dot(left_basis.T, gradient), right_basis)
    second = beta_two * exp_avg_sq + (1.0 - beta_two) * rotated * rotated
    direction = (beta_one * turned + (1.0 - beta_one) * rotated) / (jnp.sqrt(second) + epsilon)
    update = fine_dot(fine_dot(left_basis, direction), right_basis.T)
    new_weight = weight * (1.0 - learn_rate * decay_rate) - learn_rate * update
    return (update, new_weight, moment, second, left_new, right_new)


def local(fits, attn_out, cotangent, gate, *arrays):
    exp_avg, left_basis, right_basis = arrays[1], arrays[5], arrays[6]
    find = fused_gradient if fits else plain_gradient
    gradient, turned = find(attn_out, cotangent, gate, exp_avg, left_basis, right_basis)
    finish = fused_finish if fits else plain_finish
    return tuple(finish(gradient, turned, *arrays))


def solution(mesh):
    spec = P("dp", "seq")
    in_specs = (spec, P(("seq", "dp"), None), P("dp", None)) + (spec,) * 7
    fits = mesh.shape["seq"] == 4 and mesh.shape["dp"] == BLOCKS
    body = functools.partial(local, fits)
    return jax.shard_map(body, mesh=mesh, in_specs=in_specs, out_specs=(spec,) * 6, check_vma=False)
```
